512 devices in a mesh: row: 16 (over x, y), col: 32 (over z, core).
Axes of the slice: x: 4, y: 4, z: 16, core: 2. Of those that a mesh axis runs over, the one named last changes fastest.
Arguments:
- tokens: float32 [512, 5120], P('col', 'row'), may hold values from -6 to 6
- w_in: float32 [5120, 20480], P('row', 'col'), may hold values from -0.078125 to 0.078125
- w_out: float32 [20480, 5120], P('col', 'row'), may hold values from -0.0390625 to 0.0390625
- out_grad: float32 [512, 5120], P('col', 'row'), may hold values from -6 to 6
Outputs:
- output: float32 [512, 5120], P('col', 'row')
- in_grad: float32 [512, 5120], P('col', 'row')
- grad_in: float32 [5120, 20480], P('row', 'col')
- grad_out: float32 [20480, 5120], P('col', 'row')
The draws below stay inside these ranges and needn't reach their ends.
All inputs are finite; a program needn't handle non-finite values.
Results may differ from the reference program's by a relative error of at most 0.000088.
Values sent between devices are 32-bit elements; how exact they have to be, the bound alone decides.
No kernel may reach another device: no remote copies, remote signals or barrier semaphores. Data moves between devices by JAX's collectives and lax.ppermute only.
A program may use at most 64 MiB of HBM per device.

```python
import math
import jax
import jax.numpy as jnp
from jax import lax

D = 5120
FF = 20480
TOKENS = 512


def steps_of(rng, extent, cuts, low, largest):
    def one(dim, shards_of):
        draws = jax.random.uniform(jax.random.fold_in(jax.random.fold_in(rng, 6), dim), (shards_of,), jnp.float32, low / len(cuts), largest / len(cuts))
        return jnp.repeat(jnp.exp(draws), extent[dim] // shards_of).reshape((-1,) + (1,) * (len(extent) - dim - 1))

    level = one(*cuts[0])
    for cut in cuts[1:]:
        level = level * one(*cut)
    return level


def bell_draw(own_key, shape, scale, limit, shards=(), dtype=jnp.bfloat16):
    level = steps_of(own_key, shape, shards, -0.22, 0.18) if shards else 1.0
    result = jax.random.normal(own_key, shape, jnp.float32) * scale * level
    return jnp.minimum(jnp.maximum(result, -limit), limit).astype(dtype)


def setup_inputs(seed: int = 0) -> dict:
    keys = jax.random.split(jax.random.key(seed), 5)
    tokens = bell_draw(keys[0], (TOKENS, D), 1.0, 6.0, ((0, 32), (1, 16)), jnp.float32)
    w_in = bell_draw(keys[1], (D, FF), D ** -0.5, 0.078125, ((0, 16), (1, 32)), jnp.float32)
    w_out = bell_draw(keys[2], (FF, D), FF ** -0.5, 0.0390625, ((0, 32), (1, 16)), jnp.float32)
    out_grad = bell_draw(keys[3], (TOKENS, D), 1.0, 6.0, ((0, 32), (1, 16)), jnp.float32)
    return dict(tokens=tokens, w_in=w_in, w_out=w_out, out_grad=out_grad)


def gelu_parts(hidden):
    coeff = math.sqrt(2.0 / math.pi)
    inner = coeff * (hidden + 0.044715 * hidden * hidden * hidden)
    tangent = jnp.tanh(inner)
    active = 0.5 * hidden * (1.0 + tangent)
    slope = 0.5 * (1.0 + tangent) + 0.5 * hidden * (1.0 - tangent * tangent) * coeff * (1.0 + 3.0 * 0.044715 * hidden * hidden)
    return (active, slope)

def matmul(left, right):
    return jnp.dot(left, right, preferred_element_type=jnp.float32, precision=lax.Precision.HIGHEST)

def reference(tokens, w_in, w_out, out_grad):
    hidden = matmul(tokens, w_in)
    active, slope = gelu_parts(hidden)
    output = matmul(active, w_out)
    act_grad = matmul(out_grad, w_out.T)
    hid_grad = act_grad * slope
    grad_out = matmul(active.T, out_grad)
    grad_in = matmul(tokens.T, hid_grad)
    in_grad = matmul(hid_grad, w_in.T)
    return (output, in_grad, grad_in, grad_out)
```

```python
import math

import jax
import jax.numpy as jnp
from jax import lax
from jax.sharding import Mesh, PartitionSpec as P

ROW = ("x", "y")
COL = ("z", "core")
SWAP = ((0, 1), (1, 0))
SIDE, DEPTH = 4, 16

EXCHANGE = ("x", "y", "core")


def place(x, y, core):
    return (x * SIDE + y) * 2 + core


ALONG_X = {c: [[place(i, j, c) for i in range(SIDE)] for j in range(SIDE)] for c in (0, 1)}
ALONG_Y = {c: [[place(j, i, c) for i in range(SIDE)] for j in range(SIDE)] for c in (0, 1)}
FIRST = ALONG_X[0] + ALONG_Y[1]
SECOND = ALONG_Y[0] + ALONG_X[1]


def exchange(value, groups):
    return lax.all_to_all(value, EXCHANGE, 0, 0, axis_index_groups=groups)


def spread(value, groups):
    return exchange(jnp.broadcast_to(value, (SIDE,) + value.shape), groups)


def gelu_parts(hidden):
    coeff = math.sqrt(2.0 / math.pi)
    inner = coeff * (hidden + 0.044715 * hidden * hidden * hidden)
    tangent = jnp.tanh(inner)
    active = 0.5 * hidden * (1.0 + tangent)
    slope = 0.5 * (1.0 + tangent) + 0.5 * hidden * (1.0 - tangent * tangent) * coeff * (
        1.0 + 3.0 * 0.044715 * hidden * hidden
    )
    return (active, slope)


def dot(left, right, left_dim, right_dim):
    return lax.dot_general(
        left,
        right,
        (((left_dim,), (right_dim,)), ((), ())),
        preferred_element_type=jnp.float32,
        precision=lax.Precision.HIGH,
    )


def on_device(tokens, w_in, w_out, out_grad):
    few, width = tokens.shape
    hid = w_in.shape[1]
    half = few * DEPTH
    total = 2 * half
    part = total // (SIDE * SIDE)

    both = jnp.concatenate([tokens, out_grad], axis=1)
    both = lax.all_gather(both, "z", axis=0, tiled=True)
    both = jnp.concatenate([both, lax.ppermute(both, "core", SWAP)], axis=0)
    tok, cot = both[:, :width], both[:, width:]

    hidden_p = dot(tok, w_in, 1, 0).reshape(SIDE, SIDE * part, hid)
    agrad_p = dot(cot, w_out, 1, 1).reshape(SIDE, SIDE * part, hid)
    sums = exchange(jnp.stack([hidden_p, agrad_p], axis=1), FIRST).sum(axis=0)
    sums = sums.reshape(2, SIDE, part, hid).transpose(1, 0, 2, 3)
    sums = exchange(sums, SECOND).sum(axis=0)

    active, slope = gelu_parts(sums[0])
    hgrad = sums[1] * slope

    full = spread(spread(jnp.stack([active, hgrad]), SECOND), FIRST)
    act = full[:, :, 0].reshape(total, hid)
    hg = full[:, :, 1].reshape(total, hid)

    res = jnp.concatenate([dot(act, w_out, 1, 0), dot(hg, w_in, 1, 1)], axis=1)
    res = res[:half] + lax.ppermute(res[half:], "core", SWAP)
    res = lax.all_to_all(res.reshape(DEPTH, few, 2 * width), "z", 0, 0).sum(axis=0)

    grad_out = dot(act, cot, 0, 0)
    grad_in = dot(tok, hg, 0, 0)
    return (res[:, :width], res[:, width:], grad_in, grad_out)


def solution(mesh):
    grid = Mesh(mesh.devices.reshape(SIDE, SIDE, DEPTH, 2), ("x", "y", "z", "core"))
    placed = (P(COL, ROW), P(ROW, COL), P(COL, ROW), P(COL, ROW))
    return jax.shard_map(
        on_device,
        mesh=grid,
        in_specs=placed,
        out_specs=(P(COL, ROW), P(COL, ROW), P(ROW, COL), P(COL, ROW)),
        check_vma=False,
    )
```

```python
import math

import jax
import jax.numpy as jnp
from jax import lax
from jax.experimental import pallas as pl
from jax.experimental.pallas import tpu as pltpu
from jax.sharding import Mesh, PartitionSpec as P

ROW = ("x", "y")
COL = ("z", "core")
SWAP = ((0, 1), (1, 0))
SIDE, DEPTH = 4, 16
ROWS = SIDE * SIDE

def gelu_parts(hidden):
    coeff = math.sqrt(2.0 / math.pi)
    inner = coeff * (hidden + 0.044715 * hidden * hidden * hidden)
    tangent = jnp.tanh(inner)
    active = 0.5 * hidden * (1.0 + tangent)
    slope = 0.5 * (1.0 + tangent) + 0.5 * hidden * (1.0 - tangent * tangent) * coeff * (
        1.0 + 3.0 * 0.044715 * hidden * hidden
    )
    return (active, slope)


def dot(left, right, left_dim, right_dim):
    return lax.dot_general(
        left,
        right,
        (((left_dim,), (right_dim,)), ((), ())),
        preferred_element_type=jnp.float32,
        precision=lax.Precision.HIGH,
    )


def halves(value):
    high = value.astype(jnp.bfloat16)
    return high, (value - high.astype(jnp.float32)).astype(jnp.bfloat16)


def dot3(left, right, dims):
    def one(a, b):
        return lax.dot_general(a, b, (dims, ((), ())), preferred_element_type=jnp.float32)

    return one(left[0], right[0]) + one(left[0], right[1]) + one(left[1], right[0])


def whole(value):
    return (value,)


def dot_f32(left, right, dims):
    return lax.dot_general(
        left[0], right[0], (dims, ((), ())), precision=lax.Precision.HIGHEST, preferred_element_type=jnp.float32
    )


def local_call(body, out_shape, *operands):
    return pl.pallas_call(
        body,
        out_shape=out_shape,
        in_specs=[pl.BlockSpec(memory_space=pltpu.VMEM)] * len(operands),
        out_specs=jax.tree.map(lambda _: pl.BlockSpec(memory_space=pltpu.VMEM), out_shape),
        compiler_params=pltpu.CompilerParams(vmem_limit_bytes=40 * 2**20),
    )(*operands)


def first_products(pieces, dot, both_ref, w_in_ref, w_out_ref, other_ref, sums_ref):
    width, hid = w_in_ref.shape
    wide = 384
    spare = jnp.zeros((wide - width, hid), jnp.float32)
    tok = pieces(both_ref[:, :wide])
    cot = pieces(both_ref[:, 2 * width - wide :])
    shape = sums_ref.shape[:1] + sums_ref.shape[3:]
    for block, (w_in, w_out) in enumerate(((w_in_ref[...], w_out_ref[...]), (other_ref[0], other_ref[1]))):
        w_in = pieces(jnp.concatenate([w_in, spare], axis=0))
        w_out = pieces(jnp.concatenate([spare, w_out], axis=0))
        sums_ref[:, 0, block] = dot(tok, w_in, ((1,), (0,))).reshape(shape)
        sums_ref[:, 1, block] = dot(cot, w_out, ((1,), (0,))).reshape(shape)


def first_body(*refs):
    core = lax.axis_index("core")

    @pl.when(core == 0)
    def _():
        first_products(whole, dot_f32, *refs)

    @pl.when(core == 1)
    def _():
        first_products(halves, dot3, *refs)


def middle_body(parts_ref, mine_ref):
    sums = parts_ref[0]
    for i in range(1, ROWS):
        sums = sums + parts_ref[i]
    active, slope = gelu_parts(sums[0])
    hgrad = sums[1] * slope
    for i in range(ROWS):
        mine_ref[i, 0] = active
        mine_ref[i, 1] = hgrad


def second_body(full_ref, w_in_ref, w_out_ref, other_ref, res_ref):
    width, hid = w_in_ref.shape
    total = res_ref.shape[0]
    out = inn = None
    for block, (w_in, w_out) in enumerate(((w_in_ref[...], w_out_ref[...]), (other_ref[0], other_ref[1]))):
        act = halves(full_ref[:, 0, block].reshape(total, hid))
        hg = halves(full_ref[:, 1, block].reshape(total, hid))
        o = dot3(halves(w_out), act, ((1,), (1,)))
        i = dot3(halves(w_in), hg, ((1,), (1,)))
        out, inn = (o, i) if block == 0 else (out + o, inn + i)
    res_ref[...] = jnp.concatenate([out, inn], axis=0).T


def last_body(parts_ref, output_ref, in_grad_ref):
    width = output_ref.shape[1]
    total = parts_ref[0]
    for i in range(1, parts_ref.shape[0]):
        total = total + parts_ref[i]
    output_ref[...] = total[:, :width]
    in_grad_ref[...] = total[:, width:]


def floats(*shape):
    return jax.ShapeDtypeStruct(shape, jnp.float32)


def on_device(tokens, w_in, w_out, out_grad):
    few, width = tokens.shape
    hid = w_in.shape[1]
    total = few * DEPTH
    part = total // ROWS

    w_out = w_out.T
    other = lax.ppermute(jnp.stack([w_in, w_out]), "core", SWAP)

    both = lax.all_gather(jnp.concatenate([tokens, out_grad], axis=1), "z", axis=0, tiled=True)

    shape = floats(ROWS, 2, 2, part, hid)
    sums = local_call(first_body, shape, both, w_in, w_out, other)
    sums = lax.all_to_all(sums, ROW, 0, 0)

    full = lax.all_to_all(local_call(middle_body, shape, sums), ROW, 0, 0)

    res = local_call(second_body, floats(total, 2 * width), full, w_in, w_out, other)
    res = lax.all_to_all(res.reshape(DEPTH, few, 2 * width), "z", 0, 0)

    acts = [full[:, 0, i].reshape(total, hid) for i in (0, 1)]
    hgs = [full[:, 1, i].reshape(total, hid) for i in (0, 1)]
    tok, cot = both[:, :width], both[:, width:]
    grads_in = [dot(tok, h, 0, 0) for h in hgs]
    grads_out = [dot(cot, a, 0, 0) for a in acts]
    grad_in = grads_in[0] + lax.ppermute(grads_in[1], "core", SWAP)
    grad_out = grads_out[0] + lax.ppermute(grads_out[1], "core", SWAP)

    output, in_grad = local_call(last_body, (floats(few, width), floats(few, width)), res)
    return (output, in_grad, grad_in, grad_out.T)


def solution(mesh):
    grid = Mesh(mesh.devices.reshape(SIDE, SIDE, DEPTH, 2), ("x", "y", "z", "core"))
    placed = (P(COL, ROW), P(ROW, COL), P(COL, ROW), P(COL, ROW))
    return jax.shard_map(
        on_device,
        mesh=grid,
        in_specs=placed,
        out_specs=(P(COL, ROW), P(COL, ROW), P(ROW, COL), P(COL, ROW)),
        check_vma=False,
    )
```

```python
import math

import jax
import jax.numpy as jnp
from jax import lax
from jax.experimental import pallas as pl
from jax.experimental.pallas import tpu as pltpu
from jax.sharding import Mesh, PartitionSpec as P

ROW = ("x", "y")
COL = ("z", "core")
SWAP = ((0, 1), (1, 0))
SIDE, DEPTH = 4, 16
ROWS = SIDE * SIDE

def gelu_parts(hidden):
    coeff = math.sqrt(2.0 / math.pi)
    inner = coeff * (hidden + 0.044715 * hidden * hidden * hidden)
    tangent = jnp.tanh(inner)
    active = 0.5 * hidden * (1.0 + tangent)
    slope = 0.5 * (1.0 + tangent) + 0.5 * hidden * (1.0 - tangent * tangent) * coeff * (
        1.0 + 3.0 * 0.044715 * hidden * hidden
    )
    return (active, slope)


def dot(left, right, left_dim, right_dim):
    return lax.dot_general(
        left,
        right,
        (((left_dim,), (right_dim,)), ((), ())),
        preferred_element_type=jnp.float32,
        precision=lax.Precision.HIGH,
    )


def halves(value):
    high = value.astype(jnp.bfloat16)
    return high, (value - high.astype(jnp.float32)).astype(jnp.bfloat16)


def stacked(value, order, axis):
    parts = halves(value)
    return jnp.concatenate([parts[i] for i in order], axis=axis)


def exact_dot(left, right):
    def thirds(value):
        high, _ = halves(value)
        return (high,) + halves(value - high.astype(jnp.float32))

    left, right = thirds(left), thirds(right)
    total = None
    for order in (4, 3, 2, 1, 0):
        for i in range(3):
            if 0 <= order - i < 3:
                term = jnp.dot(left[i], right[order - i], preferred_element_type=jnp.float32)
                total = term if total is None else total + term
    return total


LEFT, RIGHT = (0, 1, 0), (0, 0, 1)


def local_call(body, out_shape, *operands):
    return pl.pallas_call(
        body,
        out_shape=out_shape,
        in_specs=[pl.BlockSpec(memory_space=pltpu.VMEM)] * len(operands),
        out_specs=jax.tree.map(lambda _: pl.BlockSpec(memory_space=pltpu.VMEM), out_shape),
        compiler_params=pltpu.CompilerParams(vmem_limit_bytes=40 * 2**20),
    )(*operands)


def first_body(both_ref, w_in_ref, w_out_ref, other_ref, sums_ref):
    width, hid = w_in_ref.shape
    wide = 384
    spare = jnp.zeros((wide - width, 2 * hid), jnp.float32)
    shape = sums_ref.shape[:1] + sums_ref.shape[3:]
    core = lax.axis_index("core")

    def weights(which):
        return jnp.concatenate([(w_in_ref, w_out_ref)[which][...], other_ref[which]], axis=1)

    def products(dot):
        tok = dot(both_ref[:, :wide], jnp.concatenate([weights(0), spare], axis=0))
        cot = dot(both_ref[:, 2 * width - wide :], jnp.concatenate([spare, weights(1)], axis=0))
        for which, result in enumerate((tok, cot)):
            for block in (0, 1):
                sums_ref[:, which, block] = result[:, block * hid : (block + 1) * hid].reshape(shape)

    @pl.when(core == 0)
    def _():
        products(exact_dot)

    @pl.when(core == 1)
    def _():
        products(lambda a, b: jnp.dot(stacked(a, LEFT, 1), stacked(b, RIGHT, 0), preferred_element_type=jnp.float32))


def middle_body(parts_ref, mine_ref):
    sums = parts_ref[0]
    for i in range(1, ROWS):
        sums = sums + parts_ref[i]
    active, slope = gelu_parts(sums[0])
    hgrad = sums[1] * slope
    for i in range(ROWS):
        mine_ref[i, 0] = active
        mine_ref[i, 1] = hgrad


def second_body(full_ref, w_in_ref, w_out_ref, other_ref, res_ref):
    total = res_ref.shape[0]
    hid = w_in_ref.shape[1]

    def product(which, w_ref):
        weights = jnp.concatenate([w_ref[...], other_ref[1 - which]], axis=1)
        rows = jnp.concatenate([full_ref[:, which, i].reshape(total, hid) for i in (0, 1)], axis=1)
        return lax.dot_general(
            stacked(weights, LEFT, 1),
            stacked(rows, RIGHT, 1),
            (((1,), (1,)), ((), ())),
            preferred_element_type=jnp.float32,
        )

    res_ref[...] = jnp.concatenate([product(0, w_out_ref), product(1, w_in_ref)], axis=0).T


def last_body(parts_ref, output_ref, in_grad_ref):
    width = output_ref.shape[1]
    total = parts_ref[0]
    for i in range(1, parts_ref.shape[0]):
        total = total + parts_ref[i]
    output_ref[...] = total[:, :width]
    in_grad_ref[...] = total[:, width:]


def floats(*shape):
    return jax.ShapeDtypeStruct(shape, jnp.float32)


def on_device(tokens, w_in, w_out, out_grad):
    few, width = tokens.shape
    hid = w_in.shape[1]
    total = few * DEPTH
    part = total // ROWS

    w_out = w_out.T
    other = lax.ppermute(jnp.stack([w_in, w_out]), "core", SWAP)

    both = lax.all_gather(jnp.concatenate([tokens, out_grad], axis=1), "z", axis=0, tiled=True)

    shape = floats(ROWS, 2, 2, part, hid)
    sums = local_call(first_body, shape, both, w_in, w_out, other)
    sums = lax.all_to_all(sums, ROW, 0, 0)

    full = lax.all_to_all(local_call(middle_body, shape, sums), ROW, 0, 0)

    res = local_call(second_body, floats(total, 2 * width), full, w_in, w_out, other)
    res = lax.all_to_all(res.reshape(DEPTH, few, 2 * width), "z", 0, 0)

    acts = [full[:, 0, i].reshape(total, hid) for i in (0, 1)]
    hgs = [full[:, 1, i].reshape(total, hid) for i in (0, 1)]
    tok, cot = both[:, :width], both[:, width:]
    grads_in = [dot(tok, h, 0, 0) for h in hgs]
    grads_out = [dot(cot, a, 0, 0) for a in acts]
    grad_in = grads_in[0] + lax.ppermute(grads_in[1], "core", SWAP)
    grad_out = grads_out[0] + lax.ppermute(grads_out[1], "core", SWAP)

    output, in_grad = local_call(last_body, (floats(few, width), floats(few, width)), res)
    return (output, in_grad, grad_in, grad_out.T)


def solution(mesh):
    grid = Mesh(mesh.devices.reshape(SIDE, SIDE, DEPTH, 2), ("x", "y", "z", "core"))
    placed = (P(COL, ROW), P(ROW, COL), P(COL, ROW), P(COL, ROW))
    return jax.shard_map(
        on_device,
        mesh=grid,
        in_specs=placed,
        out_specs=(P(COL, ROW), P(COL, ROW), P(ROW, COL), P(COL, ROW)),
        check_vma=False,
    )
```

```python
import math

import jax
import jax.numpy as jnp
from jax import lax
from jax.experimental import pallas as pl
from jax.experimental.pallas import tpu as pltpu
from jax.sharding import Mesh, PartitionSpec as P

ROW = ("x", "y")
COL = ("z", "core")
SWAP = ((0, 1), (1, 0))
SIDE, DEPTH = 4, 16
ROWS = SIDE * SIDE
ROW_RING = [(i + 5) % ROWS for i in range(ROWS)]
RING = [(i + 12) % DEPTH for i in range(DEPTH)]


def gelu_parts(hidden):
    coeff = math.sqrt(2.0 / math.pi)
    inner = coeff * (hidden + 0.044715 * hidden * hidden * hidden)
    tangent = jnp.tanh(inner)
    active = 0.5 * hidden * (1.0 + tangent)
    slope = 0.5 * (1.0 + tangent) + 0.5 * hidden * (1.0 - tangent * tangent) * coeff * (
        1.0 + 3.0 * 0.044715 * hidden * hidden
    )
    return (active, slope)


def dot(left, right, left_dim, right_dim):
    return lax.dot_general(
        left,
        right,
        (((left_dim,), (right_dim,)), ((), ())),
        preferred_element_type=jnp.float32,
        precision=lax.Precision.HIGH,
    )


def halves(value):
    high = value.astype(jnp.bfloat16)
    return high, (value - high.astype(jnp.float32)).astype(jnp.bfloat16)


def stacked(value, order, axis):
    parts = halves(value)
    return jnp.concatenate([parts[i] for i in order], axis=axis)


def exact_dot(left, right):
    def thirds(value):
        high, _ = halves(value)
        return (high,) + halves(value - high.astype(jnp.float32))

    left, right = thirds(left), thirds(right)
    total = None
    for order in (4, 3, 2, 1, 0):
        for i in range(3):
            if 0 <= order - i < 3:
                term = jnp.dot(left[i], right[order - i], preferred_element_type=jnp.float32)
                total = term if total is None else total + term
    return total


LEFT, RIGHT = (0, 1, 0), (0, 0, 1)


def local_call(body, out_shape, *operands):
    return pl.pallas_call(
        body,
        out_shape=out_shape,
        in_specs=[pl.BlockSpec(memory_space=pltpu.VMEM)] * len(operands),
        out_specs=jax.tree.map(lambda _: pl.BlockSpec(memory_space=pltpu.VMEM), out_shape),
        compiler_params=pltpu.CompilerParams(vmem_limit_bytes=40 * 2**20),
    )(*operands)


def first_body(both_ref, w_in_ref, w_out_ref, other_ref, sums_ref):
    width, hid = w_in_ref.shape
    wide = 384
    spare = jnp.zeros((wide - width, 2 * hid), jnp.float32)
    shape = sums_ref.shape[:1] + sums_ref.shape[3:]
    core = lax.axis_index("core")

    def weights(which):
        return jnp.concatenate([(w_in_ref, w_out_ref)[which][...], other_ref[which]], axis=1)

    def products(dot):
        tok = dot(both_ref[:, :wide], jnp.concatenate([weights(0), spare], axis=0))
        cot = dot(both_ref[:, 2 * width - wide :], jnp.concatenate([spare, weights(1)], axis=0))
        for which, result in enumerate((tok, cot)):
            for block in (0, 1):
                sums_ref[:, which, block] = result[:, block * hid : (block + 1) * hid].reshape(shape)

    @pl.when(core == 0)
    def _():
        products(exact_dot)

    @pl.when(core == 1)
    def _():
        products(lambda a, b: jnp.dot(stacked(a, LEFT, 1), stacked(b, RIGHT, 0), preferred_element_type=jnp.float32))


def middle_body(parts_ref, mine_ref):
    sums = parts_ref[0]
    for i in range(1, ROWS):
        sums = sums + parts_ref[i]
    active, slope = gelu_parts(sums[0])
    hgrad = sums[1] * slope
    for i in range(ROWS):
        mine_ref[i, 0] = active
        mine_ref[i, 1] = hgrad


def second_body(full_ref, w_in_ref, w_out_ref, other_ref, res_ref):
    total = res_ref.shape[0]
    hid = w_in_ref.shape[1]

    def product(which, w_ref):
        weights = jnp.concatenate([w_ref[...], other_ref[1 - which]], axis=1)
        rows = jnp.concatenate([full_ref[:, which, i].reshape(total, hid) for i in (0, 1)], axis=1)
        return lax.dot_general(
            stacked(weights, LEFT, 1),
            stacked(rows, RIGHT, 1),
            (((1,), (1,)), ((), ())),
            preferred_element_type=jnp.float32,
        )

    res_ref[...] = jnp.concatenate([product(0, w_out_ref), product(1, w_in_ref)], axis=0).T


def last_body(parts_ref, output_ref, in_grad_ref):
    width = output_ref.shape[1]
    total = parts_ref[0]
    for i in range(1, parts_ref.shape[0]):
        total = total + parts_ref[i]
    output_ref[...] = total[:, :width]
    in_grad_ref[...] = total[:, width:]


def floats(*shape):
    return jax.ShapeDtypeStruct(shape, jnp.float32)


def on_device(tokens, w_in, w_out, out_grad):
    few, width = tokens.shape
    hid = w_in.shape[1]
    total = few * DEPTH
    part = total // ROWS

    w_out = w_out.T
    other = lax.ppermute(jnp.stack([w_in, w_out]), "core", SWAP)

    both = lax.all_gather(jnp.concatenate([tokens, out_grad], axis=1), "z", axis=0, tiled=True, axis_index_groups=[RING])

    shape = floats(ROWS, 2, 2, part, hid)
    sums = local_call(first_body, shape, both, w_in, w_out, other)
    sums = lax.all_to_all(sums, ROW, 0, 0, axis_index_groups=[ROW_RING])

    full = lax.all_to_all(local_call(middle_body, shape, sums), ROW, 0, 0, axis_index_groups=[ROW_RING])

    res = local_call(second_body, floats(total, 2 * width), full, w_in, w_out, other)
    res = lax.all_to_all(res.reshape(DEPTH, few, 2 * width), "z", 0, 0, axis_index_groups=[RING])

    acts = [full[:, 0, i].reshape(total, hid) for i in (0, 1)]
    hgs = [full[:, 1, i].reshape(total, hid) for i in (0, 1)]
    tok, cot = both[:, :width], both[:, width:]
    grads_in = [dot(tok, h, 0, 0) for h in hgs]
    grads_out = [dot(cot, a, 0, 0) for a in acts]
    grad_in = grads_in[0] + lax.ppermute(grads_in[1], "core", SWAP)
    grad_out = grads_out[0] + lax.ppermute(grads_out[1], "core", SWAP)

    output, in_grad = local_call(last_body, (floats(few, width), floats(few, width)), res)
    return (output, in_grad, grad_in, grad_out.T)


def solution(mesh):
    grid = Mesh(mesh.devices.reshape(SIDE, SIDE, DEPTH, 2), ("x", "y", "z", "core"))
    placed = (P(COL, ROW), P(ROW, COL), P(COL, ROW), P(COL, ROW))
    return jax.shard_map(
        on_device,
        mesh=grid,
        in_specs=placed,
        out_specs=(P(COL, ROW), P(COL, ROW), P(ROW, COL), P(COL, ROW)),
        check_vma=False,
    )
```

```python
import math

import jax
import jax.numpy as jnp
from jax import lax
from jax.experimental import pallas as pl
from jax.experimental.pallas import tpu as pltpu
from jax.sharding import Mesh, PartitionSpec as P

ROW = ("x", "y")
COL = ("z", "core")
SWAP = ((0, 1), (1, 0))
SIDE, DEPTH = 4, 16
ROWS = SIDE * SIDE
ROW_RING = [(i + 5) % ROWS for i in range(ROWS)]
RING = [(i + 12) % DEPTH for i in range(DEPTH)]

PAIRS = [(2 * z + c, 2 * ((z + (1 if z % 2 == c else -1)) % DEPTH) + c) for z in range(DEPTH) for c in (0, 1)]


def gelu_parts(hidden):
    coeff = math.sqrt(2.0 / math.pi)
    inner = coeff * (hidden + 0.044715 * hidden * hidden * hidden)
    tangent = jnp.tanh(inner)
    active = 0.5 * hidden * (1.0 + tangent)
    slope = 0.5 * (1.0 + tangent) + 0.5 * hidden * (1.0 - tangent * tangent) * coeff * (
        1.0 + 3.0 * 0.044715 * hidden * hidden
    )
    return (active, slope)


def dot(left, right, left_dim, right_dim):
    return lax.dot_general(
        left,
        right,
        (((left_dim,), (right_dim,)), ((), ())),
        preferred_element_type=jnp.float32,
        precision=lax.Precision.HIGH,
    )


def halves(value):
    high = value.astype(jnp.bfloat16)
    return high, (value - high.astype(jnp.float32)).astype(jnp.bfloat16)


def stacked(value, order, axis):
    parts = halves(value)
    return jnp.concatenate([parts[i] for i in order], axis=axis)


def exact_dot(left, right):
    def thirds(value):
        high, _ = halves(value)
        return (high,) + halves(value - high.astype(jnp.float32))

    left, right = thirds(left), thirds(right)
    total = None
    for order in (4, 3, 2, 1, 0):
        for i in range(3):
            if 0 <= order - i < 3:
                term = jnp.dot(left[i], right[order - i], preferred_element_type=jnp.float32)
                total = term if total is None else total + term
    return total


LEFT, RIGHT = (0, 1, 0), (0, 0, 1)


def local_call(body, out_shape, *operands):
    return pl.pallas_call(
        body,
        out_shape=out_shape,
        in_specs=[pl.BlockSpec(memory_space=pltpu.VMEM)] * len(operands),
        out_specs=jax.tree.map(lambda _: pl.BlockSpec(memory_space=pltpu.VMEM), out_shape),
        compiler_params=pltpu.CompilerParams(vmem_limit_bytes=40 * 2**20),
    )(*operands)


def first_body(both_ref, w_in_ref, w_out_ref, other_ref, sums_ref):
    width, hid = w_in_ref.shape
    wide = 384
    spare = jnp.zeros((wide - width, 2 * hid), jnp.float32)
    shape = sums_ref.shape[:1] + sums_ref.shape[3:]
    core = lax.axis_index("core")

    def weights(which):
        return jnp.concatenate([(w_in_ref, w_out_ref)[which][...], other_ref[which]], axis=1)

    def products(dot):
        tok = dot(both_ref[:, :wide], jnp.concatenate([weights(0), spare], axis=0))
        cot = dot(both_ref[:, 2 * width - wide :], jnp.concatenate([spare, weights(1)], axis=0))
        for which, result in enumerate((tok, cot)):
            for block in (0, 1):
                sums_ref[:, which, block] = result[:, block * hid : (block + 1) * hid].reshape(shape)

    @pl.when(core == 0)
    def _():
        products(exact_dot)

    @pl.when(core == 1)
    def _():
        products(lambda a, b: jnp.dot(stacked(a, LEFT, 1), stacked(b, RIGHT, 0), preferred_element_type=jnp.float32))


def middle_body(parts_ref, mine_ref):
    sums = parts_ref[0]
    for i in range(1, ROWS):
        sums = sums + parts_ref[i]
    active, slope = gelu_parts(sums[0])
    hgrad = sums[1] * slope
    for i in range(ROWS):
        mine_ref[i, 0] = active
        mine_ref[i, 1] = hgrad


def second_body(full_ref, w_in_ref, w_out_ref, other_ref, keep_ref, send_ref):
    n, few, _ = keep_ref.shape
    total = 2 * n * few
    hid = w_in_ref.shape[1]

    def product(which, w_ref):
        weights = jnp.concatenate([w_ref[...], other_ref[1 - which]], axis=1)
        rows = jnp.concatenate([full_ref[:, which, i].reshape(total, hid) for i in (0, 1)], axis=1)
        return lax.dot_general(
            stacked(weights, LEFT, 1),
            stacked(rows, RIGHT, 1),
            (((1,), (1,)), ((), ())),
            preferred_element_type=jnp.float32,
        )

    res = jnp.concatenate([product(0, w_out_ref), product(1, w_in_ref)], axis=0).T.reshape(n, 2, few, -1)
    odd = lax.axis_index("z") % 2 == 1
    keep_ref[...] = jnp.where(odd, res[:, 1], res[:, 0])
    send_ref[...] = jnp.where(odd, res[:, 0], res[:, 1])


def last_body(parts_ref, output_ref, in_grad_ref):
    width = output_ref.shape[1]
    total = parts_ref[0]
    for i in range(1, parts_ref.shape[0]):
        total = total + parts_ref[i]
    output_ref[...] = total[:, :width]
    in_grad_ref[...] = total[:, width:]


def floats(*shape):
    return jax.ShapeDtypeStruct(shape, jnp.float32)


def on_device(tokens, w_in, w_out, out_grad):
    few, width = tokens.shape
    hid = w_in.shape[1]
    total = few * DEPTH
    part = total // ROWS

    w_out = w_out.T
    other = lax.ppermute(jnp.stack([w_in, w_out]), "core", SWAP)

    both = lax.all_gather(jnp.concatenate([tokens, out_grad], axis=1), "z", axis=0, tiled=True, axis_index_groups=[RING])

    shape = floats(ROWS, 2, 2, part, hid)
    sums = local_call(first_body, shape, both, w_in, w_out, other)
    sums = lax.all_to_all(sums, ROW, 0, 0, axis_index_groups=[ROW_RING])

    full = lax.all_to_all(local_call(middle_body, shape, sums), ROW, 0, 0, axis_index_groups=[ROW_RING])

    block = floats(DEPTH // 2, few, 2 * width)
    keep, send = local_call(second_body, (block, block), full, w_in, w_out, other)
    res = keep + lax.ppermute(send, COL, PAIRS)
    res = lax.all_to_all(res, "z", 0, 0, axis_index_groups=[RING[0::2], RING[1::2]])

    acts = [full[:, 0, i].reshape(total, hid) for i in (0, 1)]
    hgs = [full[:, 1, i].reshape(total, hid) for i in (0, 1)]
    tok, cot = both[:, :width], both[:, width:]
    grads_in = [dot(tok, h, 0, 0) for h in hgs]
    grads_out = [dot(cot, a, 0, 0) for a in acts]
    grad_in = grads_in[0] + lax.ppermute(grads_in[1], "core", SWAP)
    grad_out = grads_out[0] + lax.ppermute(grads_out[1], "core", SWAP)

    output, in_grad = local_call(last_body, (floats(few, width), floats(few, width)), res)
    return (output, in_grad, grad_in, grad_out.T)


def solution(mesh):
    grid = Mesh(mesh.devices.reshape(SIDE, SIDE, DEPTH, 2), ("x", "y", "z", "core"))
    placed = (P(COL, ROW), P(ROW, COL), P(COL, ROW), P(COL, ROW))
    return jax.shard_map(
        on_device,
        mesh=grid,
        in_specs=placed,
        out_specs=(P(COL, ROW), P(COL, ROW), P(ROW, COL), P(COL, ROW)),
        check_vma=False,
    )
```
